512 devices in a mesh: chan: 8 (over y_hi, core), dp: 64 (over z, x, y_lo).
Axes of the slice: x: 4, y: 8 (y_hi: 4, y_lo: 2; y = y_hi * 2 + y_lo), z: 8, core: 2. Of those that a mesh axis runs over, the one named last changes fastest.
Arguments:
- volume: bfloat16 [128, 32, 32, 256], P('dp', None, None, 'chan'), may hold values from -6 to 6
- filter_one: bfloat16 [3, 3, 3, 256, 256], P(None, None, None, 'chan'), may hold values from -0.078125 to 0.078125
- filter_two: bfloat16 [3, 3, 3, 256, 256], P(None, None, None, 'chan'), may hold values from -0.078125 to 0.078125
- cotangent: bfloat16 [128, 32, 32, 256], P('dp', None, None, 'chan'), may hold values from -6 to 6
Outputs:
- output: bfloat16 [128, 32, 32, 256], P('dp', None, None, 'chan')
- input_grad: bfloat16 [128, 32, 32, 256], P('dp', None, None, 'chan')
- grad_one: float32 [3, 3, 3, 256, 256], P(None, None, None, 'chan')
- grad_two: float32 [3, 3, 3, 256, 256], P(None, None, None, 'chan')
The draws below stay inside these ranges and needn't reach their ends.
All inputs are finite; a program needn't handle non-finite values.
Results may differ from the reference program's by a relative error of at most 0.02525.
The reference program's roundings to bfloat16 on the way (of `act_one`, `delta_two` and `delta_one`) count: a program that leaves them out, or rounds other values in their place, can miss the bound.
Values may be sent and summed in bfloat16 or wider, within the bound.
A program may use at most 128 MiB of HBM per device.

```python
import math
import jax
import jax.numpy as jnp
from jax import lax

C = 256
VOX = 32
ROWS = 128
SAMPLES = 4


def block_levels(own_key, extent, cuts, smallest, high):
    factor_of = 1.0
    for axis_at, shards_of in cuts:
        steps = jax.random.uniform(jax.random.fold_in(jax.random.fold_in(own_key, 6), axis_at), (shards_of,), jnp.float32, smallest / len(cuts), high / len(cuts))
        factor_of = factor_of * jnp.repeat(jnp.exp(steps), extent[axis_at] // shards_of).reshape((-1,) + (1,) * (len(extent) - 1 - axis_at))
    return factor_of


def scatter_about(rng, extent, scale, limit, shards=(), dtype=jnp.bfloat16):
    loudness = block_levels(rng, extent, shards, -0.22, 0.18) if shards else 1.0
    drawn = jax.random.normal(rng, extent, jnp.float32) * scale * loudness
    return jnp.minimum(jnp.maximum(drawn, -limit), limit).astype(dtype)


def setup_inputs(seed: int = 0) -> dict:
    keys = jax.random.split(jax.random.key(seed), 5)
    volume = scatter_about(keys[0], (ROWS, VOX, VOX, C), 1.0, 6.0, ((0, 64), (3, 8)))
    filter_one = scatter_about(keys[1], (3, 3, 3, C, C), (27 * C) ** -0.5, 0.078125, ((3, 8),))
    filter_two = scatter_about(keys[2], (3, 3, 3, C, C), (27 * C) ** -0.5, 0.078125, ((3, 8),))
    cotangent = scatter_about(keys[3], (ROWS, VOX, VOX, C), 1.0, 6.0, ((0, 64), (3, 8)))
    return dict(volume=volume, filter_one=filter_one, filter_two=filter_two, cotangent=cotangent)


SLOPE = 0.3

def leaky(values):
    return jnp.where(values > 0, values, SLOPE * values)

def slope_of(values):
    return jnp.where(values > 0, jnp.float32(1.0), jnp.float32(SLOPE))

def padded(cubes):
    return jnp.pad(cubes.astype(jnp.float32), ((0, 0), (1, 1), (1, 1), (1, 1), (0, 0)))

def conv(cubes, weight):
    samples, depth, height, width_w, inner = cubes.shape
    source = padded(cubes)
    weights = weight.astype(jnp.float32)
    total = jnp.zeros((samples * depth * height * width_w, weight.shape[4]), jnp.float32)
    for a in range(3):
        for b in range(3):
            for c in range(3):
                piece = source[:, a:a + depth, b:b + height, c:c + width_w, :].reshape(-1, inner)
                total = total + jnp.dot(piece, weights[a, b, c], precision=lax.Precision.HIGHEST)
    return total

def conv_back(delta, weight):
    samples, depth, height, width_w, outer = delta.shape
    source = padded(delta)
    weights = weight.astype(jnp.float32)
    total = jnp.zeros((samples * depth * height * width_w, weight.shape[3]), jnp.float32)
    for a in range(3):
        for b in range(3):
            for c in range(3):
                piece = source[:, 2 - a:2 - a + depth, 2 - b:2 - b + height, 2 - c:2 - c + width_w, :].reshape(-1, outer)
                total = total + jnp.dot(piece, weights[a, b, c].T, precision=lax.Precision.HIGHEST)
    return total

def filter_grad(cubes, delta):
    samples, depth, height, width_w, inner = cubes.shape
    source = padded(cubes)
    flat = delta.astype(jnp.float32).reshape(-1, delta.shape[4])
    taps = []
    for a in range(3):
        for b in range(3):
            for c in range(3):
                piece = source[:, a:a + depth, b:b + height, c:c + width_w, :].reshape(-1, inner)
                taps.append(jnp.dot(piece.T, flat, precision=lax.Precision.HIGHEST))
    return jnp.stack(taps).reshape(3, 3, 3, inner, flat.shape[1])

def reference(volume, filter_one, filter_two, cotangent):
    shape = (SAMPLES, VOX, VOX, VOX, C)
    cubes = jnp.roll(volume, -1, axis=0).reshape(shape)
    cot = jnp.roll(cotangent, -1, axis=0)
    scale = 1.0 / math.sqrt(SAMPLES * VOX * VOX * VOX)
    pre_one = conv(cubes, filter_one)
    act_one = leaky(pre_one).astype(jnp.bfloat16)
    pre_two = conv(act_one.reshape(shape), filter_two)
    output = leaky(pre_two).astype(jnp.bfloat16)
    delta_two = (cot.reshape(-1, C).astype(jnp.float32) * slope_of(pre_two)).astype(jnp.bfloat16)
    grad_two = filter_grad(act_one.reshape(shape), delta_two.reshape(shape)) * scale
    back_two = conv_back(delta_two.reshape(shape), filter_two)
    delta_one = (back_two * slope_of(pre_one)).astype(jnp.bfloat16)
    grad_one = filter_grad(cubes, delta_one.reshape(shape)) * scale
    input_grad = conv_back(delta_one.reshape(shape), filter_one).astype(jnp.bfloat16)
    output = jnp.roll(output.reshape(volume.shape), 1, axis=0)
    input_grad = jnp.roll(input_grad.reshape(volume.shape), 1, axis=0)
    return (output, input_grad, grad_one, grad_two)
```

```python
import functools
import math

import jax
import jax.numpy as jnp
from jax import lax
from jax.experimental import pallas as pl
from jax.experimental.pallas import tpu as pltpu
from jax.sharding import PartitionSpec as P

MESH = pl.DeviceIdType.MESH
SLOPE = 0.3
X, Y, Z = 4, 8, 8
N = 32
C = 256
HW = 1024
TAPS = 27
RP = 896
PART = RP // Z
SCALE = 1.0 / math.sqrt(4 * 32 * 32 * 32)
BF = jnp.bfloat16
F32 = jnp.float32


def shifted(x, rows, cols):
    pos = lax.broadcasted_iota(jnp.int32, x.shape, 1)
    off = rows * 32 + cols
    if off == 0:
        return x
    y = pltpu.roll(x, (-off) % HW, 1)
    ok = None
    if rows == 1:
        ok = pos < HW - 32
    if rows == -1:
        ok = pos >= 32
    if cols == 1:
        ok = (pos % 32) != 31
    if cols == -1:
        ok = (pos % 32) != 0
    return jnp.where(ok, y, jnp.zeros_like(y))


class Net:
    def __init__(self):
        chan = lax.axis_index("chan")
        dp = lax.axis_index("dp")
        self.c = chan
        self.core = chan % 2
        self.yl = dp % 2
        self.y = (chan // 2) * 2 + self.yl
        self.q = dp // 2
        self.x = self.q % X
        self.z = self.q // X
        self.dp = dp

    def dev(self, q, y, core):
        return {"chan": (y // 2) * 2 + core, "dp": q * 2 + y % 2}

    def in_ring(self, t, core):
        return self.dev(self.q, (self.y + t + Y) % Y, core)


class Copies:
    def __init__(self, send, recv, base):
        self.send, self.recv, self.next = send, recv, base
        self.started = []

    def slot(self):
        k = self.next
        self.next += 1
        return k

    def start(self, k, src, dst, device):
        cp = pltpu.make_async_remote_copy(
            src_ref=src,
            dst_ref=dst,
            send_sem=self.send.at[k],
            recv_sem=self.recv.at[k],
            device_id=device,
            device_id_type=MESH,
        )
        cp.start()
        self.started.append(cp)

    def wait(self, k, dst, device):
        pltpu.make_async_remote_copy(
            src_ref=dst,
            dst_ref=dst,
            send_sem=self.send.at[k],
            recv_sem=self.recv.at[k],
            device_id=device,
            device_id_type=MESH,
        ).wait_recv()

    def drain(self):
        for cp in self.started:
            cp.wait_send()
        self.started = []


def main_block(e, y, core):
    c = (y // 2) * 2 + core
    return e.at[pl.ds(1 + 2 * (y % 2), 2), pl.ds(pl.multiple_of(c * N, N), N), :]


def one_plane(e, plane, y, core):
    c = (y // 2) * 2 + core
    return e.at[pl.ds(plane, 1), pl.ds(pl.multiple_of(c * N, N), N), :]


def halo_block(e, y, core):
    return one_plane(e, 5 - 5 * (y % 2), y, core)


class Gather:
    def __init__(self, net, copies, e):
        self.net, self.cp, self.e = net, copies, e
        s = copies.slot
        self.k = {}
        for d in (1, -1):
            for t in (1, 2, 3, 4):
                self.k["main", d, t] = s()
                self.k["main", d, t, "sib"] = s()
            for t in (1, 2, 3):
                self.k["halo", d, t] = s()
                if t != 2:
                    self.k["halo", d, t, "sib"] = s()
        self.k["halo"] = s()
        self.k["own"] = s()

    def origin(self, d, t):
        return (self.net.y - d * t + Y) % Y

    def piece(self, kind, d, t, core):
        y = self.origin(d, t)
        if kind == "halo":
            return halo_block(self.e, y, core)
        if t == 4:
            plane = 1 + 2 * (y % 2) + (0 if d == 1 else 1)
            return one_plane(self.e, plane, y, core)
        return main_block(self.e, y, core)

    def send_on(self, kind, d, t, core):
        y = self.origin(d, t - 1)
        if kind == "halo":
            ref = halo_block(self.e, y, core)
        elif t == 4:
            plane = 1 + 2 * (y % 2) + (0 if d == 1 else 1)
            ref = one_plane(self.e, plane, y, core)
        else:
            ref = main_block(self.e, y, core)
        self.cp.start(self.k[kind, d, t], ref, ref, self.net.in_ring(d, core))

    def start(self):
        n, e = self.net, self.e
        step = 2 * n.yl - 1
        q = (n.q + step + X * Z) % (X * Z)
        self.far = n.dev(q, n.y, n.core)
        self.cp.start(
            self.k["halo"],
            one_plane(e, 1 + 3 * n.yl, n.y, n.core),
            halo_block(e, n.y, n.core),
            n.dev(q, n.y, n.core),
        )
        self.send_on("main", 1, 1, n.core)
        self.send_on("main", -1, 1, n.core)
        own = main_block(e, n.y, n.core)
        self.cp.start(self.k["own"], own, own, n.in_ring(0, 1 - n.core))

    def got(self, kind, d, t):
        n = self.net
        ref = self.piece(kind, d, t, n.core)
        self.cp.wait(self.k[kind, d, t], ref, n.in_ring(-d, n.core))
        if t < (3 if kind == "halo" else 4):
            self.send_on(kind, d, t + 1, n.core)
        if kind == "main" or t != 2:
            self.cp.start(self.k[kind, d, t, "sib"], ref, ref, n.in_ring(0, 1 - n.core))

    def run(self):
        n = self.net
        both = (1, -1)
        for d in both:
            self.got("main", d, 1)
        ref = halo_block(self.e, n.y, n.core)
        self.cp.wait(self.k["halo"], ref, self.far)
        for d in both:
            self.send_on("halo", d, 1, n.core)
        for t in (2, 3, 4):
            for d in both:
                self.got("main", d, t)
            for d in both:
                self.got("halo", d, t - 1)
        sib = n.in_ring(0, 1 - n.core)
        other = 1 - n.core
        self.cp.wait(self.k["own"], main_block(self.e, n.y, other), sib)
        for d in both:
            for t in (1, 2, 3, 4):
                self.cp.wait(self.k["main", d, t, "sib"], self.piece("main", d, t, other), sib)
            for t in (1, 3):
                self.cp.wait(self.k["halo", d, t, "sib"], self.piece("halo", d, t, other), sib)
        self.cp.drain()


class Turn:
    def __init__(self, net, copies, src, dst):
        self.net, self.cp, self.src, self.dst = net, copies, src, dst
        self.k = {(t, rc): copies.slot() for t in (1, 2, 3) for rc in (0, 1)}
        self.k[0] = copies.slot()

    def rows(self, c):
        return self.dst.at[pl.ds(pl.multiple_of(c * N, N), N), :]

    def start(self):
        n = self.net
        way = 2 * n.yl - 1
        for t in (1, 2, 3):
            y = (n.y + way * t + Y) % Y
            for rc in (0, 1):
                core = (n.core + rc) % 2
                c = (y // 2) * 2 + core
                self.cp.start(self.k[t, rc], self.src.at[c], self.rows(n.c), n.dev(n.q, y, core))
        other = (n.y // 2) * 2 + 1 - n.core
        self.cp.start(self.k[0], self.src.at[other], self.rows(n.c), n.in_ring(0, 1 - n.core))
        self.dst[pl.ds(pl.multiple_of(n.c * N, N), N), :] = self.src[n.c]

    def finish(self):
        n = self.net
        way = 2 * n.yl - 1
        for t in (1, 2, 3):
            y = (n.y + (way * t if t != 2 else -way * t) + Y) % Y
            for rc in (0, 1):
                core = (n.core + rc) % 2
                c = (y // 2) * 2 + core
                self.cp.wait(self.k[t, rc], self.rows(c), n.dev(n.q, y, core))
        other = (n.y // 2) * 2 + 1 - n.core
        self.cp.wait(self.k[0], self.rows(other), n.in_ring(0, 1 - n.core))
        self.cp.drain()


class Reduce:
    def __init__(self, net, copies, part, r1, b2, r2, s2, x4, fin, out):
        self.net, self.cp = net, copies
        self.part, self.r1, self.b2, self.r2, self.s2 = part, r1, b2, r2, s2
        self.x4, self.fin, self.out = x4, fin, out
        self.ka = [copies.slot() for _ in range(Z - 1)]
        self.kb = copies.slot()
        self.kc = [copies.slot() for _ in range(X - 1)]
        self.kd = copies.slot()
        self.ke = [copies.slot() for _ in range(Z - 1)]

    def zdev(self, t):
        n = self.net
        return n.dev(((n.z + t + Z) % Z) * X + n.x, n.y, n.core)

    def xdev(self, t):
        n = self.net
        return n.dev(n.z * X + (n.x + t + X) % X, n.y, n.core)

    def pair(self):
        n = self.net
        return n.dev(n.q, n.y + 1 - 2 * n.yl, n.core)

    def start(self):
        n = self.net
        for t in range(1, Z):
            self.cp.start(self.ka[t - 1], self.part.at[(n.z + t) % Z], self.r1.at[t - 1], self.zdev(t))

    def sum_z(self):
        n = self.net
        total = self.part[n.z].astype(F32)
        for t in range(1, Z):
            self.cp.wait(self.ka[t - 1], self.r1.at[t - 1], self.zdev(-t))
            total = total + self.r1[t - 1].astype(F32)
        for h in (0, 1):
            half = total[:, h * 128 : (h + 1) * 128]
            self.s2[h] = half
            self.b2[h] = half.astype(BF)
        self.cp.start(self.kb, self.b2.at[1 - n.yl], self.r2, self.pair())

    def sum_y(self):
        n = self.net
        self.cp.wait(self.kb, self.r2, self.pair())
        self.x4[n.x] = (self.s2[n.yl] + self.r2[...].astype(F32)).astype(BF)
        for t in range(1, X):
            self.cp.start(self.kc[t - 1], self.x4.at[n.x], self.x4.at[n.x], self.xdev(t))

    def sum_x(self):
        n = self.net
        for t in range(1, X):
            self.cp.wait(self.kc[t - 1], self.x4.at[(n.x - t + X) % X], self.xdev(-t))
        total = self.x4[0].astype(F32)
        for x in range(1, X):
            total = total + self.x4[x].astype(F32)
        self.fin[n.z, n.yl] = total.astype(BF)
        ref = self.fin.at[n.z, n.yl]
        self.cp.start(self.kd, ref, ref, self.pair())

    def spread(self):
        n = self.net
        self.cp.wait(self.kd, self.fin.at[n.z, 1 - n.yl], self.pair())
        for t in range(1, Z):
            self.cp.start(self.ke[t - 1], self.fin.at[n.z], self.fin.at[n.z], self.zdev(t))

    def finish(self):
        n = self.net
        for t in range(1, Z):
            self.cp.wait(self.ke[t - 1], self.fin.at[(n.z - t + Z) % Z], self.zdev(-t))
        for z in range(Z):
            rows = min(PART, TAPS * N - z * PART)
            for h in (0, 1):
                self.out[z * PART : z * PART + rows, h * 128 : (h + 1) * 128] = (
                    self.fin[z, h, :rows].astype(F32) * SCALE
                )
        self.cp.drain()


def conv(w, e, base, s, sign, use):
    for j in (0, 1):

        @pl.loop(0, HW // 256)
        def _(t):
            lanes = pl.ds(pl.multiple_of(t * 256, 256), 256)
            planes = e[pl.ds(base + j, 3), :, lanes].reshape(3 * C, 256)
            s[:, lanes] = jnp.dot(w[j], planes, preferred_element_type=F32)

        total = None
        for c in range(3):
            line = None
            for b in range(3):
                at = (b * 3 + c) * N
                term = shifted(s[at : at + N, :], sign * (b - 1), 0)
                line = term if line is None else line + term
            line = shifted(line, 0, sign * (c - 1))
            total = line if total is None else total + line
        use(j, total)


def grad_columns(e, c, base, joined, a):
    for slot in range(4):
        plane = e[base + slot, pl.ds(pl.multiple_of(c * N, N), N), :].astype(F32)
        for col in range(3):
            moved = shifted(plane, 0, col - 1)
            for row in range(3):
                value = shifted(moved, row - 1, 0)
                for j in (0, 1):
                    depth = slot - j
                    if 0 <= depth < 3:
                        v = value * joined if (j, depth) in ((0, 2), (1, 0)) else value
                        at = (depth * 9 + row * 3 + col) * N
                        a[j, at : at + N, :] = v.astype(BF)


def grad_part(a, e, base, part):
    nt = (((1,), (1,)), ((), ()))
    one = e[base + 1]
    two = e[base + 2]
    for z in range(Z):
        rows = min(PART, TAPS * N - z * PART)
        at = slice(z * PART, z * PART + rows)
        g = lax.dot_general(a[0, at], one, nt, preferred_element_type=F32)
        g = g + lax.dot_general(a[1, at], two, nt, preferred_element_type=F32)
        part[z, :rows] = g.astype(BF)
        if rows < PART:
            part[z, rows:] = jnp.zeros((PART - rows, C), BF)


def filter_rows(block, joined, at, w):
    lanes = slice(at * C, (at + 1) * C)
    masked = (block.astype(F32) * joined).astype(BF)
    w[0, :, lanes] = masked if at == 2 else block
    w[1, :, lanes] = masked if at == 0 else block


def forward_filter(turned, joined, w):
    rows = turned[...].astype(F32).T
    for a in range(3):
        filter_rows(rows[a * 288 : (a + 1) * 288].astype(BF), joined, a, w)


def backward_filter(own, joined, w):
    for a in range(3):
        filter_rows(own[(2 - a) * 288 : (3 - a) * 288, :], joined, a, w)


def whole(
    vol, cot, own1, own2, out1, out2,
    output, input_grad, g1, g2,
    e1, e2, e3, e4, t1, t2, wf1, wf2, wb1, wb2, s, pre, a, part1, part2,
    r1, b2, r2, s2, x4, fin, send, recv,
):
    net = Net()
    barrier = pltpu.get_barrier_semaphore()
    greeted = [net.in_ring(t, core) for t in range(1, Y) for core in (0, 1)]
    greeted.append(net.in_ring(0, 1 - net.core))
    total = X * Z
    for t in range(1, Z):
        greeted.append(net.dev(((net.z + t) % Z) * X + net.x, net.y, net.core))
    for t in range(1, X):
        greeted.append(net.dev(net.z * X + (net.x + t) % X, net.y, net.core))
    for t in (1, -1):
        greeted.append(net.dev((net.q + t + total) % total, net.y, net.core))
    for device in greeted:
        pl.semaphore_signal(barrier, inc=1, device_id=device, device_id_type=MESH)
    pl.semaphore_wait(barrier, len(greeted))

    base = 2 * net.yl
    joined = jnp.where(net.dp % 16 == 0, 0.0, 1.0).astype(F32)

    def own(e):
        return pl.ds(pl.multiple_of(net.c * N, N), N)

    even, odd = Copies(send, recv, 0), Copies(send, recv, 29)
    turn1 = Turn(net, Copies(send, recv, 58), out1, t1)
    turn2 = Turn(net, Copies(send, recv, 65), out2, t2)
    gathers = []
    for i, e in enumerate((e1, e2, e3, e4)):
        gathers.append(Gather(net, Copies(send, recv, (i % 2) * 29), e))
    red2 = Reduce(net, Copies(send, recv, 72), part2, r1.at[1], b2.at[1], r2.at[1], s2.at[1], x4.at[1], fin.at[1], g2)
    red1 = Reduce(net, Copies(send, recv, 91), part1, r1.at[0], b2.at[0], r2.at[0], s2.at[0], x4.at[0], fin.at[0], g1)

    for j in (0, 1):
        e1[base + 1 + j, own(e1), :] = vol[j]
    turn1.start()
    gathers[0].start()
    backward_filter(own1, joined, wb1)
    backward_filter(own2, joined, wb2)
    gathers[0].run()
    turn1.finish()
    turn2.start()
    forward_filter(t1, joined, wf1)

    def after_one(j, v):
        pre[j] = jnp.where(v > 0, jnp.float32(1.0), jnp.float32(SLOPE))
        e2[base + 1 + j, own(e2), :] = jnp.where(v > 0, v, SLOPE * v).astype(BF)

    conv(wf1, e1, base, s, 1, after_one)

    gathers[1].start()
    gathers[1].run()
    turn2.finish()
    forward_filter(t2, joined, wf2)

    def after_two(j, v):
        output[j] = jnp.where(v > 0, v, SLOPE * v).astype(BF)
        slope = jnp.where(v > 0, jnp.float32(1.0), jnp.float32(SLOPE))
        e3[base + 1 + j, own(e3), :] = (cot[j].astype(F32) * slope).astype(BF)

    conv(wf2, e2, base, s, 1, after_two)

    gathers[2].start()
    grad_columns(e2, net.c, base, joined, a)
    gathers[2].run()

    def after_back(j, v):
        e4[base + 1 + j, own(e4), :] = (v * pre[j]).astype(BF)

    conv(wb2, e3, base, s, -1, after_back)

    gathers[3].start()
    grad_part(a, e3, base, part2)
    red2.start()
    grad_columns(e1, net.c, base, joined, a)
    gathers[3].run()
    red2.sum_z()
    grad_part(a, e4, base, part1)
    red1.start()
    red2.sum_y()

    def last(j, v):
        input_grad[j] = v.astype(BF)

    conv(wb1, e4, base, s, -1, last)
    red2.sum_x()
    red1.sum_z()
    red2.spread()
    red1.sum_y()
    red1.sum_x()
    red2.finish()
    red1.spread()
    red1.finish()


def local(volume, filter_one, filter_two, cotangent):
    def planes(v):
        return v.transpose(0, 3, 1, 2).reshape(2, N, HW)

    def back(v):
        return v.reshape(2, N, 32, 32).transpose(0, 2, 3, 1)

    def by_owner(w):
        w = w.reshape(TAPS, N, 8, N).transpose(2, 1, 0, 3).reshape(8, N, TAPS * N)
        return jnp.pad(w, ((0, 0), (0, 0), (0, RP - TAPS * N)))

    vm = pl.BlockSpec(memory_space=pltpu.VMEM)
    shape = jax.ShapeDtypeStruct
    output, input_grad, g1, g2 = pl.pallas_call(
        whole,
        out_shape=(
            shape((2, N, HW), BF),
            shape((2, N, HW), BF),
            shape((TAPS * N, C), F32),
            shape((TAPS * N, C), F32),
        ),
        in_specs=[vm] * 6,
        out_specs=[vm] * 4,
        scratch_shapes=[
            pltpu.VMEM((6, C, HW), BF),
            pltpu.VMEM((6, C, HW), BF),
            pltpu.VMEM((6, C, HW), BF),
            pltpu.VMEM((6, C, HW), BF),
            pltpu.VMEM((C, RP), BF),
            pltpu.VMEM((C, RP), BF),
            pltpu.VMEM((2, 288, 3 * C), BF),
            pltpu.VMEM((2, 288, 3 * C), BF),
            pltpu.VMEM((2, 288, 3 * C), BF),
            pltpu.VMEM((2, 288, 3 * C), BF),
            pltpu.VMEM((288, HW), F32),
            pltpu.VMEM((2, N, HW), F32),
            pltpu.VMEM((2, TAPS * N, HW), BF),
            pltpu.VMEM((Z, PART, C), BF),
            pltpu.VMEM((Z, PART, C), BF),
            pltpu.VMEM((2, Z - 1, PART, C), BF),
            pltpu.VMEM((2, 2, PART, 128), BF),
            pltpu.VMEM((2, PART, 128), BF),
            pltpu.VMEM((2, 2, PART, 128), F32),
            pltpu.VMEM((2, X, PART, 128), BF),
            pltpu.VMEM((2, Z, 2, PART, 128), BF),
            pltpu.SemaphoreType.DMA((110,)),
            pltpu.SemaphoreType.DMA((110,)),
        ],
        compiler_params=pltpu.CompilerParams(
            collective_id=0, has_side_effects=True, vmem_limit_bytes=50 * 1024 * 1024
        ),
    )(
        planes(volume),
        planes(cotangent),
        filter_one.reshape(TAPS * N, C),
        filter_two.reshape(TAPS * N, C),
        by_owner(filter_one),
        by_owner(filter_two),
    )
    filters = (3, 3, 3, N, C)
    return back(output), back(input_grad), g1.reshape(filters), g2.reshape(filters)


def solution(mesh):
    rows = P("dp", None, None, "chan")
    filters = P(None, None, None, "chan", None)
    return jax.shard_map(
        local,
        mesh=mesh,
        in_specs=(rows, filters, filters, rows),
        out_specs=(rows, rows, filters, filters),
        check_vma=False,
    )
```

```python
import functools
import math

import jax
import jax.numpy as jnp
from jax import lax
from jax.experimental import pallas as pl
from jax.experimental.pallas import tpu as pltpu
from jax.sharding import PartitionSpec as P

MESH = pl.DeviceIdType.MESH
SLOPE = 0.3
X, Y, Z = 4, 8, 8
N = 32
C = 256
HW = 1024
TAPS = 27
SHARE = 7
SCALE = 1.0 / math.sqrt(4 * 32 * 32 * 32)
BF = jnp.bfloat16
F32 = jnp.float32


def shifted(x, rows, cols):
    pos = lax.broadcasted_iota(jnp.int32, x.shape, 1)
    off = rows * 32 + cols
    if off == 0:
        return x
    y = pltpu.roll(x, (-off) % HW, 1)
    ok = None
    if rows == 1:
        ok = pos < HW - 32
    if rows == -1:
        ok = pos >= 32
    if cols == 1:
        ok = (pos % 32) != 31
    if cols == -1:
        ok = (pos % 32) != 0
    return jnp.where(ok, y, jnp.zeros_like(y))


class Net:
    def __init__(self):
        chan = lax.axis_index("chan")
        dp = lax.axis_index("dp")
        self.c = chan
        self.core = chan % 2
        self.yl = dp % 2
        self.y = (chan // 2) * 2 + self.yl
        self.q = dp // 2
        self.x = self.q % X
        self.z = self.q // X
        self.dp = dp

    def dev(self, q, y, core):
        return {"chan": (y // 2) * 2 + core, "dp": q * 2 + y % 2}

    def xdev(self, t):
        return self.dev(self.z * X + (self.x + t + X) % X, self.y, self.core)

    def zdev(self, t):
        return self.dev(((self.z + t + Z) % Z) * X + self.x, self.y, self.core)

    def in_ring(self, t, core):
        return self.dev(self.q, (self.y + t + Y) % Y, core)


class Copies:
    def __init__(self, send, recv, base):
        self.send, self.recv, self.next = send, recv, base
        self.started = []

    def slot(self):
        k = self.next
        self.next += 1
        return k

    def start(self, k, src, dst, device):
        cp = pltpu.make_async_remote_copy(
            src_ref=src,
            dst_ref=dst,
            send_sem=self.send.at[k],
            recv_sem=self.recv.at[k],
            device_id=device,
            device_id_type=MESH,
        )
        cp.start()
        self.started.append(cp)

    def wait(self, k, dst, device):
        pltpu.make_async_remote_copy(
            src_ref=dst,
            dst_ref=dst,
            send_sem=self.send.at[k],
            recv_sem=self.recv.at[k],
            device_id=device,
            device_id_type=MESH,
        ).wait_recv()

    def drain(self):
        for cp in self.started:
            cp.wait_send()
        self.started = []


def block(e, slot, y, core):
    c = (y // 2) * 2 + core
    return e.at[slot, pl.ds(pl.multiple_of(c * N, N), N), :]


class Gather:
    BOTH = (1, -1)

    def __init__(self, net, copies, e):
        self.net, self.cp, self.e = net, copies, e
        self.k = {}
        s = copies.slot
        for kind in ("outer", "inner"):
            self.k[kind] = s()
            for d in self.BOTH:
                for t in (1, 2, 3, 4):
                    if t < 4 or (kind == "outer") == (d == 1):
                        self.k[kind, d, t] = s()
                        if kind == "inner" or t % 2 == 0:
                            self.k[kind, d, t, "sib"] = s()
                    if kind == "outer" and t % 2 == 1:
                        self.k["far", d, t] = s()
                        self.k["far", d, t, "sib"] = s()

    def at(self, kind, d, t, core):
        y = (self.net.y - d * t + Y) % Y
        if kind == "far":
            return block(self.e, 5 * self.net.yl, y, core)
        return block(self.e, 1 + 3 * (y % 2) if kind == "outer" else 2 + y % 2, y, core)

    def sibling(self):
        return self.net.in_ring(0, 1 - self.net.core)

    def pass_on(self, kind, d, t):
        ref = self.at(kind, d, t - 1, self.net.core)
        self.cp.start(self.k[kind, d, t], ref, ref, self.net.in_ring(d, self.net.core))

    def start(self, kinds=("inner", "outer")):
        for kind in kinds:
            for d in self.BOTH:
                self.pass_on(kind, d, 1)
            ref = self.at(kind, 1, 0, self.net.core)
            self.cp.start(self.k[kind], ref, ref, self.sibling())

    def share(self, kind, d, t):
        ref = self.at(kind, d, t, self.net.core)
        self.cp.start(self.k[kind, d, t, "sib"], ref, ref, self.sibling())

    def got(self, kind, d, t):
        n = self.net
        ref = self.at(kind, d, t, n.core)
        self.cp.wait(self.k[kind, d, t], ref, n.in_ring(-d, n.core))
        if (kind, d, t + 1) in self.k:
            self.pass_on(kind, d, t + 1)
        if kind == "outer" and t % 2 == 1:
            q = (n.q + 1 - 2 * n.yl + X * Z) % (X * Z)
            self.cp.start(self.k["far", d, t], ref, self.at("far", d, t, n.core), n.dev(q, n.y, n.core))
        if (kind, d, t, "sib") in self.k:
            self.share(kind, d, t)

    def far(self, t):
        n = self.net
        q = (n.q - 1 + 2 * n.yl + X * Z) % (X * Z)
        for d in self.BOTH:
            self.cp.wait(self.k["far", d, t], self.at("far", d, t, n.core), n.dev(q, n.y, n.core))
            self.share("far", d, t)

    def step(self, t):
        for kind in ("inner", "outer"):
            for d in self.BOTH:
                if (kind, d, t) in self.k:
                    self.got(kind, d, t)
        if t >= 3:
            self.far(2 * t - 5)

    def most(self):
        other = 1 - self.net.core
        for kind in ("inner", "outer"):
            self.cp.wait(self.k[kind], self.at(kind, 1, 0, other), self.sibling())
        self.from_sibling(("inner", "outer"))

    def from_sibling(self, kinds):
        for key in self.k:
            if len(key) == 4 and key[0] in kinds:
                self.cp.wait(self.k[key], self.at(*key[:3], 1 - self.net.core), self.sibling())

    def rest(self):
        self.from_sibling(("far",))


class Turn:
    def __init__(self, net, copies, src, dst, me, shares, peer):
        self.net, self.cp, self.src, self.dst = net, copies, src, dst
        self.me, self.shares, self.peer = me, shares, peer
        self.k = {(t, rc): copies.slot() for t in (1, 2, 3) for rc in (0, 1)}
        self.k[0] = copies.slot()
        self.kp = [copies.slot() for _ in range(shares - 1)]

    def rows(self, c):
        return self.dst.at[self.me, pl.ds(pl.multiple_of(c * N, N), N), :]

    def cut(self, own):
        lanes = self.src.shape[2]
        count = lanes // N
        pos = lax.broadcasted_iota(jnp.int32, (N, lanes), 1) // N
        made = [None] * 8
        for k in range(count):
            tap = jnp.minimum(self.me * count + k, TAPS - 1)
            v = own[pl.ds(pl.multiple_of(tap * N, N), N), :].astype(F32)
            for c in range(8):
                r = pltpu.roll(v, ((k - c) % 8) * N, 1) if k != c else v
                r = r[:, :lanes]
                made[c] = r if k == 0 else jnp.where(pos == k, r, made[c])
        for c in range(8):
            self.src[c] = made[c].astype(BF)

    def start(self):
        n = self.net
        way = 2 * n.yl - 1
        for t in (1, 2, 3):
            y = (n.y + way * t + Y) % Y
            for rc in (0, 1):
                core = (n.core + rc) % 2
                c = (y // 2) * 2 + core
                self.cp.start(self.k[t, rc], self.src.at[c], self.rows(n.c), n.dev(n.q, y, core))
        other = (n.y // 2) * 2 + 1 - n.core
        self.cp.start(self.k[0], self.src.at[other], self.rows(n.c), n.in_ring(0, 1 - n.core))
        self.dst[self.me, pl.ds(pl.multiple_of(n.c * N, N), N), :] = self.src[n.c]

    def spread(self):
        n = self.net
        way = 2 * n.yl - 1
        for t in (1, 2, 3):
            y = (n.y + (way * t if t != 2 else -way * t) + Y) % Y
            for rc in (0, 1):
                core = (n.core + rc) % 2
                c = (y // 2) * 2 + core
                self.cp.wait(self.k[t, rc], self.rows(c), n.dev(n.q, y, core))
        other = (n.y // 2) * 2 + 1 - n.core
        self.cp.wait(self.k[0], self.rows(other), n.in_ring(0, 1 - n.core))
        ref = self.dst.at[self.me]
        for t in range(1, self.shares):
            self.cp.start(self.kp[t - 1], ref, ref, self.peer(t))

    def finish(self):
        for t in range(1, self.shares):
            ref = self.dst.at[(self.me - t + self.shares) % self.shares]
            self.cp.wait(self.kp[t - 1], ref, self.peer(-t))
        self.cp.drain()

    def filters(self, joined, w):
        count = self.src.shape[2] // N
        for share in range(-(-TAPS // count)):
            rows = self.dst[share].astype(F32).T
            for k in range(min(count, TAPS - share * count)):
                tap = share * count + k
                filter_rows(rows[k * N : (k + 1) * N], joined, tap // 9, (tap % 9) * N, w)


class Reduce:
    def __init__(self, net, copies, part, r1, p2, r2, q, rq, fin, out):
        self.net, self.cp = net, copies
        self.part, self.r1, self.p2, self.r2 = part, r1, p2, r2
        self.q, self.rq, self.fin, self.out = q, rq, fin, out
        self.others = [(t, h) for t in range(Z) for h in (0, 1) if (t, h) != (0, 0)]
        self.ka = [copies.slot() for _ in range(X - 1)]
        self.kb = [copies.slot() for _ in self.others]
        self.kc = [copies.slot() for _ in range(8)]
        self.kd = [copies.slot() for _ in range(Z - 1)]
        self.ke = [copies.slot() for _ in range(X - 1)]

    def peer(self, t, h):
        n = self.net
        y = n.y + (h - 2 * h * n.yl)
        return n.dev(((n.z + t + Z) % Z) * X + n.x, y, n.core)

    def start(self):
        n = self.net
        for t in range(1, X):
            src = self.part.at[(n.x + t) % X]
            self.cp.start(self.ka[t - 1], src, self.r1.at[t - 1], n.xdev(t))

    def sum_x(self):
        n = self.net
        for t in range(1, X):
            self.cp.wait(self.ka[t - 1], self.r1.at[t - 1], n.xdev(-t))
        total = self.part[n.x].astype(F32)
        for t in range(1, X):
            total = total + self.r1[t - 1].astype(F32)
        for z in range(SHARE):
            for h in (0, 1):
                self.p2[z, h] = total[z * N : (z + 1) * N, h * 128 : (h + 1) * 128].astype(BF)
        for i, (t, h) in enumerate(self.others):
            src = self.p2.at[(n.z + t) % Z, (n.yl + h) % 2]
            self.cp.start(self.kb[i], src, self.r2.at[i], self.peer(t, h))

    def turns(self):
        n = self.net
        for h in (0, 1):
            for m in range(4):
                c = 4 * n.yl + m
                yield h, m, c, {"chan": c, "dp": n.q * 2 + (n.yl + h) % 2}

    def turn_copy(self, h, m, device):
        return pltpu.make_async_remote_copy(
            src_ref=self.q.at[pl.ds(m * N, N), :],
            dst_ref=self.rq.at[self.net.c],
            send_sem=self.cp.send.at[self.kc[4 * h + m]],
            recv_sem=self.cp.recv.at[self.kc[0] + self.net.c],
            device_id=device,
            device_id_type=MESH,
        )

    def sum_z(self):
        n = self.net
        for i, (t, h) in enumerate(self.others):
            self.cp.wait(self.kb[i], self.r2.at[i], self.peer(-t, h))
        total = self.p2[n.z, n.yl].astype(F32)
        for i in range(len(self.others)):
            total = total + self.r2[i].astype(F32)
        square = jnp.concatenate([total, jnp.zeros((128 - N, 128), F32)], axis=0)
        self.q[...] = square.T.astype(BF)
        for h, m, c, device in self.turns():
            if h:
                self.turn_copy(h, m, device).start()
                continue

            @pl.when(c != n.c)
            def _():
                self.turn_copy(h, m, device).start()

            @pl.when(c == n.c)
            def _():
                self.rq[n.c] = self.q[m * N : (m + 1) * N, :]

    def collect(self):
        n = self.net
        half = n.c // 4
        for c in range(8):

            @pl.when(jnp.logical_or(c != n.c, half != n.yl))
            def _():
                self.cp.wait(self.kc[c], self.rq.at[c], {"chan": c, "dp": n.q * 2 + half})

        for h, m, c, device in self.turns():
            if h:
                self.turn_copy(h, m, device).wait_send()
                continue

            @pl.when(c != n.c)
            def _():
                self.turn_copy(h, m, device).wait_send()

        for h in (0, 1):
            total = self.rq[4 * h].astype(F32)
            for k in (1, 2, 3):
                total = total + pltpu.roll(self.rq[4 * h + k].astype(F32), k * N, 1)
            self.fin[n.x, n.z, :, h * 128 : (h + 1) * 128] = total.astype(BF)
        ref = self.fin.at[n.x, n.z]
        for t in range(1, Z):
            self.cp.start(self.kd[t - 1], ref, ref, n.zdev(t))

    def spread(self):
        n = self.net
        for t in range(1, Z):
            self.cp.wait(self.kd[t - 1], self.fin.at[n.x, (n.z - t + Z) % Z], n.zdev(-t))
        ref = self.fin.at[n.x, pl.ds(0, SHARE)]
        for t in range(1, X):
            self.cp.start(self.ke[t - 1], ref, ref, n.xdev(t))

    def finish(self):
        n = self.net
        for t in range(1, X):
            ref = self.fin.at[(n.x - t + X) % X, pl.ds(0, SHARE)]
            self.cp.wait(self.ke[t - 1], ref, n.xdev(-t))
        for tap in range(TAPS):
            self.out[tap * N : (tap + 1) * N, :] = self.fin[tap // SHARE, tap % SHARE].astype(F32) * SCALE
        self.cp.drain()


def conv(w, e, base, s, sign, j):
    @pl.loop(0, HW // 256)
    def _(t):
        lanes = pl.ds(pl.multiple_of(t * 256, 256), 256)
        planes = e[pl.ds(base + j, 3), :, lanes].reshape(3 * C, 256)
        s[:, lanes] = jnp.dot(w[j], planes, preferred_element_type=F32)

    total = None
    for c in range(3):
        line = None
        for b in range(3):
            at = (b * 3 + c) * N
            term = shifted(s[at : at + N, :], sign * (b - 1), 0)
            line = term if line is None else line + term
        line = shifted(line, 0, sign * (c - 1))
        total = line if total is None else total + line
    return total


def grad_columns(e, c, base, a):
    for j in (0, 1):
        plane = e[base + 1 + j, pl.ds(pl.multiple_of(c * N, N), N), :].astype(F32)
        for col in range(3):
            moved = shifted(plane, 0, 1 - col)
            for row in range(3):
                at = (row * 3 + col) * N
                a[j, at : at + N, :] = shifted(moved, 1 - row, 0).astype(BF)


def grad_part(a, e, base, joined, depth, part):
    nt = (((1,), (1,)), ((), ()))
    one = lax.dot_general(a[0], e[base + depth], nt, preferred_element_type=F32)
    two = lax.dot_general(a[1], e[base + depth + 1], nt, preferred_element_type=F32)
    if depth == 2:
        one = one * joined
    if depth == 0:
        two = two * joined
    g = one + two
    for k in range(9):
        tap = depth * 9 + k
        part[tap // SHARE, pl.ds((tap % SHARE) * N, N), :] = g[k * N : (k + 1) * N].astype(BF)


def filter_rows(rows, joined, depth, at, w):
    count = rows.shape[0]
    lanes = slice(depth * C, (depth + 1) * C)
    plain = rows.astype(BF)
    masked = (rows * joined).astype(BF)
    w[0, at : at + count, lanes] = masked if depth == 2 else plain
    w[1, at : at + count, lanes] = masked if depth == 0 else plain


def backward_filter(own, joined, w):
    for a in range(3):
        filter_rows(own[(2 - a) * 288 : (3 - a) * 288, :].astype(F32), joined, a, 0, w)


def whole(
    vol, cot, own1, own2,
    output, input_grad, g1, g2,
    e1, e2, e3, e4, w1, w2, t1, t2, wf1, wf2, wb1, wb2, s, pre, a1, a2, part1, part2,
    r1, p2, r2, q, rq, fin, send, recv,
):
    net = Net()
    barrier = pltpu.get_barrier_semaphore()
    greeted = [net.in_ring(t, core) for t in range(1, Y) for core in (0, 1)]
    greeted.append(net.in_ring(0, 1 - net.core))
    total = X * Z
    for t in range(1, Z):
        greeted.append(net.zdev(t))
        greeted.append(net.dev(((net.z + t) % Z) * X + net.x, net.y + 1 - 2 * net.yl, net.core))
    for t in range(1, X):
        greeted.append(net.xdev(t))
    for t in (1, -1):
        greeted.append(net.dev((net.q + t + total) % total, net.y, net.core))
    for device in greeted:
        pl.semaphore_signal(barrier, inc=1, device_id=device, device_id_type=MESH)

    base = 2 * net.yl
    joined = jnp.where(net.dp % 16 == 0, 0.0, 1.0).astype(F32)

    def own(e):
        return pl.ds(pl.multiple_of(net.c * N, N), N)

    gathers = []
    for i, e in enumerate((e1, e2, e3, e4)):
        cp = Copies(send, recv, (i % 2) * SEMS_GATHER)
        gathers.append(Gather(net, cp, e))
        assert cp.next == (i % 2 + 1) * SEMS_GATHER
    cp = Copies(send, recv, 2 * SEMS_GATHER)
    turn1 = Turn(net, cp, w1, t1, net.x, X, net.xdev)
    cp = Copies(send, recv, cp.next)
    turn2 = Turn(net, cp, w2, t2, net.z, Z, net.zdev)
    cp = Copies(send, recv, cp.next)
    red2 = Reduce(net, cp, part2, r1.at[1], p2.at[1], r2.at[1], q.at[1], rq.at[1], fin.at[1], g2)
    cp = Copies(send, recv, cp.next)
    red1 = Reduce(net, cp, part1, r1.at[0], p2.at[0], r2.at[0], q.at[0], rq.at[0], fin.at[0], g1)
    assert cp.next <= SEMS

    for j in (0, 1):
        e1[base + 1 + j, own(e1), :] = vol[j]
        p2[j, SHARE] = jnp.zeros((2, N, 128), BF)
    for part in (part1, part2):
        part[X - 1, pl.ds((SHARE - 1) * N, N), :] = jnp.zeros((N, C), BF)
    turn1.cut(own1)
    turn2.cut(own2)
    pl.semaphore_wait(barrier, len(greeted))
    inner, outer = 1 - net.yl, net.yl
    kinds = ((inner, "inner"), (outer, "outer"))
    turn1.start()
    gathers[0].start()
    turn2.start()
    gathers[0].step(1)
    backward_filter(own2, joined, wb2)
    gathers[0].step(2)
    turn1.spread()
    backward_filter(own1, joined, wb1)
    gathers[0].step(3)
    turn2.spread()
    gathers[0].step(4)
    turn1.finish()
    turn1.filters(joined, wf1)
    gathers[0].most()
    for j, kind in kinds:
        if kind == "outer":
            gathers[0].rest()
        v = conv(wf1, e1, base, s, 1, j)
        e2[base + 1 + j, own(e2), :] = jnp.where(v > 0, v, SLOPE * v).astype(BF)
        gathers[1].start((kind,))
        pre[j] = jnp.where(v > 0, jnp.float32(1.0), jnp.float32(SLOPE))
    gathers[0].cp.drain()

    gathers[1].step(1)
    gathers[1].step(2)
    turn2.finish()
    gathers[1].step(3)
    turn2.filters(joined, wf2)
    gathers[1].step(4)
    gathers[1].most()
    for j, kind in kinds:
        if kind == "outer":
            gathers[1].rest()
        v = conv(wf2, e2, base, s, 1, j)
        slope = jnp.where(v > 0, jnp.float32(1.0), jnp.float32(SLOPE))
        e3[base + 1 + j, own(e3), :] = (cot[j].astype(F32) * slope).astype(BF)
        gathers[2].start((kind,))
        output[j] = jnp.where(v > 0, v, SLOPE * v).astype(BF)
    gathers[1].cp.drain()

    grad_columns(e3, net.c, base, a2)
    gathers[2].step(1)
    grad_part(a2, e2, base, joined, 0, part2)
    gathers[2].step(2)
    grad_part(a2, e2, base, joined, 1, part2)
    gathers[2].step(3)
    grad_part(a2, e2, base, joined, 2, part2)
    red2.start()
    gathers[2].step(4)
    gathers[2].most()
    for j, kind in kinds:
        if kind == "outer":
            gathers[2].rest()
        v = conv(wb2, e3, base, s, -1, j)
        e4[base + 1 + j, own(e4), :] = (v * pre[j]).astype(BF)
        gathers[3].start((kind,))
    gathers[2].cp.drain()

    grad_columns(e4, net.c, base, a1)
    for depth in range(3):
        grad_part(a1, e1, base, joined, depth, part1)
    red1.start()
    gathers[3].step(1)
    red2.sum_x()
    gathers[3].step(2)
    red1.sum_x()
    gathers[3].step(3)
    red2.sum_z()
    red1.sum_z()
    gathers[3].step(4)
    red1.collect()
    red2.collect()
    gathers[3].most()
    input_grad[inner] = conv(wb1, e4, base, s, -1, inner).astype(BF)
    gathers[3].rest()
    red1.spread()
    red2.spread()
    input_grad[outer] = conv(wb1, e4, base, s, -1, outer).astype(BF)
    gathers[3].cp.drain()
    red2.finish()
    red1.finish()


SEMS_GATHER = 34
SEMS = 2 * SEMS_GATHER + 10 + 14 + 2 * 36


def local(volume, filter_one, filter_two, cotangent):
    def planes(v):
        return v.transpose(0, 3, 1, 2).reshape(2, N, HW)

    def back(v):
        return v.reshape(2, N, 32, 32).transpose(0, 2, 3, 1)

    vm = pl.BlockSpec(memory_space=pltpu.VMEM)
    shape = jax.ShapeDtypeStruct
    output, input_grad, g1, g2 = pl.pallas_call(
        whole,
        out_shape=(
            shape((2, N, HW), BF),
            shape((2, N, HW), BF),
            shape((TAPS * N, C), F32),
            shape((TAPS * N, C), F32),
        ),
        in_specs=[vm] * 4,
        out_specs=[vm] * 4,
        scratch_shapes=[
            pltpu.VMEM((6, C, HW), BF),
            pltpu.VMEM((6, C, HW), BF),
            pltpu.VMEM((6, C, HW), BF),
            pltpu.VMEM((6, C, HW), BF),
            pltpu.VMEM((8, N, C), BF),
            pltpu.VMEM((8, N, 128), BF),
            pltpu.VMEM((X, C, C), BF),
            pltpu.VMEM((Z, C, 128), BF),
            pltpu.VMEM((2, 288, 3 * C), BF),
            pltpu.VMEM((2, 288, 3 * C), BF),
            pltpu.VMEM((2, 288, 3 * C), BF),
            pltpu.VMEM((2, 288, 3 * C), BF),
            pltpu.VMEM((288, HW), F32),
            pltpu.VMEM((2, N, HW), F32),
            pltpu.VMEM((2, 288, HW), BF),
            pltpu.VMEM((2, 288, HW), BF),
            pltpu.VMEM((X, SHARE * N, C), BF),
            pltpu.VMEM((X, SHARE * N, C), BF),
            pltpu.VMEM((2, X - 1, SHARE * N, C), BF),
            pltpu.VMEM((2, Z, 2, N, 128), BF),
            pltpu.VMEM((2, 2 * Z - 1, N, 128), BF),
            pltpu.VMEM((2, 128, 128), BF),
            pltpu.VMEM((2, 8, N, 128), BF),
            pltpu.VMEM((2, X, Z, N, C), BF),
            pltpu.SemaphoreType.DMA((SEMS,)),
            pltpu.SemaphoreType.DMA((SEMS,)),
        ],
        compiler_params=pltpu.CompilerParams(
            collective_id=0, has_side_effects=True, vmem_limit_bytes=50 * 1024 * 1024
        ),
    )(
        planes(volume),
        planes(cotangent),
        filter_one.reshape(TAPS * N, C),
        filter_two.reshape(TAPS * N, C),
    )
    filters = (3, 3, 3, N, C)
    return back(output), back(input_grad), g1.reshape(filters), g2.reshape(filters)


def solution(mesh):
    rows = P("dp", None, None, "chan")
    filters = P(None, None, None, "chan", None)
    return jax.shard_map(
        local,
        mesh=mesh,
        in_specs=(rows, filters, filters, rows),
        out_specs=(rows, rows, filters, filters),
        check_vma=False,
    )
```

```python
import functools
import math

import jax
import jax.numpy as jnp
from jax import lax
from jax.experimental import pallas as pl
from jax.experimental.pallas import tpu as pltpu
from jax.sharding import PartitionSpec as P

MESH = pl.DeviceIdType.MESH
SLOPE = 0.3
X, Y, Z = 4, 8, 8
N = 32
C = 256
HW = 1024
TAPS = 27
SHARE = 7
SCALE = 1.0 / math.sqrt(4 * 32 * 32 * 32)
BF = jnp.bfloat16
F32 = jnp.float32


def shifted(x, rows, cols):
    pos = lax.broadcasted_iota(jnp.int32, x.shape, 1)
    off = rows * 32 + cols
    if off == 0:
        return x
    y = pltpu.roll(x, (-off) % HW, 1)
    ok = None
    if rows == 1:
        ok = pos < HW - 32
    if rows == -1:
        ok = pos >= 32
    if cols == 1:
        ok = (pos % 32) != 31
    if cols == -1:
        ok = (pos % 32) != 0
    return jnp.where(ok, y, jnp.zeros_like(y))


class Net:
    def __init__(self):
        chan = lax.axis_index("chan")
        dp = lax.axis_index("dp")
        self.c = chan
        self.core = chan % 2
        self.yl = dp % 2
        self.y = (chan // 2) * 2 + self.yl
        self.q = dp // 2
        self.x = self.q % X
        self.z = self.q // X
        self.dp = dp

    def dev(self, q, y, core):
        return {"chan": (y // 2) * 2 + core, "dp": q * 2 + y % 2}

    def xdev(self, t):
        return self.dev(self.z * X + (self.x + t + X) % X, self.y, self.core)

    def zdev(self, t):
        return self.dev(((self.z + t + Z) % Z) * X + self.x, self.y, self.core)

    def in_ring(self, t, core):
        return self.dev(self.q, (self.y + t + Y) % Y, core)


class Copies:
    def __init__(self, send, recv, base):
        self.send, self.recv, self.next = send, recv, base
        self.started = []

    def slot(self):
        k = self.next
        self.next += 1
        return k

    def start(self, k, src, dst, device):
        cp = pltpu.make_async_remote_copy(
            src_ref=src,
            dst_ref=dst,
            send_sem=self.send.at[k],
            recv_sem=self.recv.at[k],
            device_id=device,
            device_id_type=MESH,
        )
        cp.start()
        self.started.append(cp)

    def wait(self, k, dst, device):
        pltpu.make_async_remote_copy(
            src_ref=dst,
            dst_ref=dst,
            send_sem=self.send.at[k],
            recv_sem=self.recv.at[k],
            device_id=device,
            device_id_type=MESH,
        ).wait_recv()

    def drain(self):
        for cp in self.started:
            cp.wait_send()
        self.started = []


def block(e, slot, y, core, half):
    c = (y // 2) * 2 + core
    return e.at[slot, pl.ds(pl.multiple_of(c * N + half * 16, 16), 16), :]


class Gather:
    BOTH = (1, -1)

    def __init__(self, net, copies, e):
        self.net, self.cp, self.e = net, copies, e
        self.k = {}
        s = copies.slot
        for kind in ("outer0", "inner0", "outer1", "inner1"):
            self.k[kind] = s()
            for d in self.BOTH:
                for t in (1, 2, 3, 4):
                    if t < 4 or (kind[:5] == "outer") == (d == 1):
                        self.k[kind, d, t] = s()
                        if kind[:5] == "inner" or t % 2 == 0:
                            self.k[kind, d, t, "sib"] = s()
                    if kind[:5] == "outer" and t % 2 == 1:
                        self.k["far" + kind[5], d, t] = s()
                        self.k["far" + kind[5], d, t, "sib"] = s()

    def at(self, kind, d, t, core):
        y = (self.net.y - d * t + Y) % Y
        half = int(kind[-1])
        if kind[:3] == "far":
            return block(self.e, 5 * self.net.yl, y, core, half)
        return block(self.e, 1 + 3 * (y % 2) if kind[:5] == "outer" else 2 + y % 2, y, core, half)

    def sibling(self):
        return self.net.in_ring(0, 1 - self.net.core)

    def pass_on(self, kind, d, t):
        ref = self.at(kind, d, t - 1, self.net.core)
        self.cp.start(self.k[kind, d, t], ref, ref, self.net.in_ring(d, self.net.core))

    def start(self, kinds=("inner", "outer")):
        for kind in [k + half for k in kinds for half in "01"]:
            for d in self.BOTH:
                self.pass_on(kind, d, 1)
            ref = self.at(kind, 1, 0, self.net.core)
            self.cp.start(self.k[kind], ref, ref, self.sibling())

    def share(self, kind, d, t):
        ref = self.at(kind, d, t, self.net.core)
        self.cp.start(self.k[kind, d, t, "sib"], ref, ref, self.sibling())

    def got(self, kind, d, t):
        n = self.net
        ref = self.at(kind, d, t, n.core)
        self.cp.wait(self.k[kind, d, t], ref, n.in_ring(-d, n.core))
        if (kind, d, t + 1) in self.k:
            self.pass_on(kind, d, t + 1)
        if kind[:5] == "outer" and t % 2 == 1:
            q = (n.q + 1 - 2 * n.yl + X * Z) % (X * Z)
            far = "far" + kind[5]
            self.cp.start(self.k[far, d, t], ref, self.at(far, d, t, n.core), n.dev(q, n.y, n.core))
        if (kind, d, t, "sib") in self.k:
            self.share(kind, d, t)

    def far(self, t):
        n = self.net
        q = (n.q - 1 + 2 * n.yl + X * Z) % (X * Z)
        for far in ("far0", "far1"):
            for d in self.BOTH:
                self.cp.wait(self.k[far, d, t], self.at(far, d, t, n.core), n.dev(q, n.y, n.core))
                self.share(far, d, t)

    def step(self, t):
        for kind in ("inner0", "inner1", "outer0", "outer1"):
            for d in self.BOTH:
                if (kind, d, t) in self.k:
                    self.got(kind, d, t)
        if t >= 3:
            self.far(2 * t - 5)

    def most(self):
        other = 1 - self.net.core
        for kind in ("inner0", "inner1", "outer0", "outer1"):
            self.cp.wait(self.k[kind], self.at(kind, 1, 0, other), self.sibling())
        self.from_sibling(("inner0", "inner1", "outer0", "outer1"))

    def from_sibling(self, kinds):
        for key in self.k:
            if len(key) == 4 and key[0] in kinds:
                self.cp.wait(self.k[key], self.at(*key[:3], 1 - self.net.core), self.sibling())

    def rest(self):
        self.from_sibling(("far0", "far1"))


class Turn:
    def __init__(self, net, copies, src, dst, me, shares, peer):
        self.net, self.cp, self.src, self.dst = net, copies, src, dst
        self.me, self.shares, self.peer = me, shares, peer
        self.k = {(t, rc): copies.slot() for t in (1, 2, 3) for rc in (0, 1)}
        self.k[0] = copies.slot()
        self.kp = [copies.slot() for _ in range(shares - 1)]

    def rows(self, c):
        return self.dst.at[self.me, pl.ds(pl.multiple_of(c * N, N), N), :]

    def cut(self, own):
        lanes = self.src.shape[2]
        count = lanes // N
        pos = lax.broadcasted_iota(jnp.int32, (N, lanes), 1) // N
        made = [None] * 8
        for k in range(count):
            tap = jnp.minimum(self.me * count + k, TAPS - 1)
            v = own[pl.ds(pl.multiple_of(tap * N, N), N), :].astype(F32)
            for c in range(8):
                r = pltpu.roll(v, ((k - c) % 8) * N, 1) if k != c else v
                r = r[:, :lanes]
                made[c] = r if k == 0 else jnp.where(pos == k, r, made[c])
        for c in range(8):
            self.src[c] = made[c].astype(BF)

    def start(self):
        n = self.net
        way = 2 * n.yl - 1
        for t in (1, 2, 3):
            y = (n.y + way * t + Y) % Y
            for rc in (0, 1):
                core = (n.core + rc) % 2
                c = (y // 2) * 2 + core
                self.cp.start(self.k[t, rc], self.src.at[c], self.rows(n.c), n.dev(n.q, y, core))
        other = (n.y // 2) * 2 + 1 - n.core
        self.cp.start(self.k[0], self.src.at[other], self.rows(n.c), n.in_ring(0, 1 - n.core))
        self.dst[self.me, pl.ds(pl.multiple_of(n.c * N, N), N), :] = self.src[n.c]

    def spread(self):
        n = self.net
        way = 2 * n.yl - 1
        for t in (1, 2, 3):
            y = (n.y + (way * t if t != 2 else -way * t) + Y) % Y
            for rc in (0, 1):
                core = (n.core + rc) % 2
                c = (y // 2) * 2 + core
                self.cp.wait(self.k[t, rc], self.rows(c), n.dev(n.q, y, core))
        other = (n.y // 2) * 2 + 1 - n.core
        self.cp.wait(self.k[0], self.rows(other), n.in_ring(0, 1 - n.core))
        ref = self.dst.at[self.me]
        for t in range(1, self.shares):
            self.cp.start(self.kp[t - 1], ref, ref, self.peer(t))

    def finish(self):
        for t in range(1, self.shares):
            ref = self.dst.at[(self.me - t + self.shares) % self.shares]
            self.cp.wait(self.kp[t - 1], ref, self.peer(-t))
        self.cp.drain()

    def filters(self, joined, w):
        count = self.src.shape[2] // N
        for share in range(-(-TAPS // count)):
            rows = self.dst[share].astype(F32).T
            for k in range(min(count, TAPS - share * count)):
                tap = share * count + k
                filter_rows(rows[k * N : (k + 1) * N], joined, tap // 9, (tap % 9) * N, w)


class Reduce:
    def __init__(self, net, copies, part, r1, p2, r2, q, rq, fin, out):
        self.net, self.cp = net, copies
        self.part, self.r1, self.p2, self.r2 = part, r1, p2, r2
        self.q, self.rq, self.fin, self.out = q, rq, fin, out
        self.others = [(t, h) for t in range(Z) for h in (0, 1) if (t, h) != (0, 0)]
        self.ka = [copies.slot() for _ in range(X - 1)]
        self.kb = [copies.slot() for _ in self.others]
        self.kc = [copies.slot() for _ in range(8)]
        self.kd = [copies.slot() for _ in range(Z - 1)]
        self.ke = [copies.slot() for _ in range(X - 1)]

    def peer(self, t, h):
        n = self.net
        y = n.y + (h - 2 * h * n.yl)
        return n.dev(((n.z + t + Z) % Z) * X + n.x, y, n.core)

    def start(self):
        n = self.net
        for t in range(1, X):
            src = self.part.at[(n.x + t) % X]
            self.cp.start(self.ka[t - 1], src, self.r1.at[t - 1], n.xdev(t))

    def sum_x(self):
        n = self.net
        for t in range(1, X):
            self.cp.wait(self.ka[t - 1], self.r1.at[t - 1], n.xdev(-t))
        total = self.part[n.x].astype(F32)
        for t in range(1, X):
            total = total + self.r1[t - 1].astype(F32)
        for z in range(SHARE):
            for h in (0, 1):
                self.p2[z, h] = total[z * N : (z + 1) * N, h * 128 : (h + 1) * 128].astype(BF)
        for i, (t, h) in enumerate(self.others):
            src = self.p2.at[(n.z + t) % Z, (n.yl + h) % 2]
            self.cp.start(self.kb[i], src, self.r2.at[i], self.peer(t, h))

    def turns(self):
        n = self.net
        for h in (0, 1):
            for m in range(4):
                c = 4 * n.yl + m
                yield h, m, c, {"chan": c, "dp": n.q * 2 + (n.yl + h) % 2}

    def turn_copy(self, h, m, device):
        return pltpu.make_async_remote_copy(
            src_ref=self.q.at[pl.ds(m * N, N), :],
            dst_ref=self.rq.at[self.net.c],
            send_sem=self.cp.send.at[self.kc[4 * h + m]],
            recv_sem=self.cp.recv.at[self.kc[0] + self.net.c],
            device_id=device,
            device_id_type=MESH,
        )

    def sum_z(self):
        n = self.net
        for i, (t, h) in enumerate(self.others):
            self.cp.wait(self.kb[i], self.r2.at[i], self.peer(-t, h))
        total = self.p2[n.z, n.yl].astype(F32)
        for i in range(len(self.others)):
            total = total + self.r2[i].astype(F32)
        square = jnp.concatenate([total, jnp.zeros((128 - N, 128), F32)], axis=0)
        self.q[...] = square.T.astype(BF)
        for h, m, c, device in self.turns():
            if h:
                self.turn_copy(h, m, device).start()
                continue

            @pl.when(c != n.c)
            def _():
                self.turn_copy(h, m, device).start()

            @pl.when(c == n.c)
            def _():
                self.rq[n.c] = self.q[m * N : (m + 1) * N, :]

    def collect(self):
        n = self.net
        half = n.c // 4
        for c in range(8):

            @pl.when(jnp.logical_or(c != n.c, half != n.yl))
            def _():
                self.cp.wait(self.kc[c], self.rq.at[c], {"chan": c, "dp": n.q * 2 + half})

        for h, m, c, device in self.turns():
            if h:
                self.turn_copy(h, m, device).wait_send()
                continue

            @pl.when(c != n.c)
            def _():
                self.turn_copy(h, m, device).wait_send()

        for h in (0, 1):
            total = self.rq[4 * h].astype(F32)
            for k in (1, 2, 3):
                total = total + pltpu.roll(self.rq[4 * h + k].astype(F32), k * N, 1)
            self.fin[n.x, n.z, :, h * 128 : (h + 1) * 128] = total.astype(BF)
        ref = self.fin.at[n.x, n.z]
        for t in range(1, Z):
            self.cp.start(self.kd[t - 1], ref, ref, n.zdev(t))

    def spread(self):
        n = self.net
        for t in range(1, Z):
            self.cp.wait(self.kd[t - 1], self.fin.at[n.x, (n.z - t + Z) % Z], n.zdev(-t))
        ref = self.fin.at[n.x, pl.ds(0, SHARE)]
        for t in range(1, X):
            self.cp.start(self.ke[t - 1], ref, ref, n.xdev(t))

    def finish(self):
        n = self.net
        for t in range(1, X):
            ref = self.fin.at[(n.x - t + X) % X, pl.ds(0, SHARE)]
            self.cp.wait(self.ke[t - 1], ref, n.xdev(-t))
        for tap in range(TAPS):
            self.out[tap * N : (tap + 1) * N, :] = self.fin[tap // SHARE, tap % SHARE].astype(F32) * SCALE
        self.cp.drain()


def conv(w, e, base, s, sign, j):
    @pl.loop(0, HW // 256)
    def _(t):
        lanes = pl.ds(pl.multiple_of(t * 256, 256), 256)
        planes = e[pl.ds(base + j, 3), :, lanes].reshape(3 * C, 256)
        s[:, lanes] = jnp.dot(w[j], planes, preferred_element_type=F32)

    total = None
    for c in range(3):
        line = None
        for b in range(3):
            at = (b * 3 + c) * N
            term = shifted(s[at : at + N, :], sign * (b - 1), 0)
            line = term if line is None else line + term
        line = shifted(line, 0, sign * (c - 1))
        total = line if total is None else total + line
    return total


def grad_columns(e, c, base, a):
    for j in (0, 1):
        plane = e[base + 1 + j, pl.ds(pl.multiple_of(c * N, N), N), :].astype(F32)
        for col in range(3):
            moved = shifted(plane, 0, 1 - col)
            for row in range(3):
                at = (row * 3 + col) * N
                a[j, at : at + N, :] = shifted(moved, 1 - row, 0).astype(BF)


def grad_part(a, e, base, joined, depth, part):
    nt = (((1,), (1,)), ((), ()))
    one = lax.dot_general(a[0], e[base + depth], nt, preferred_element_type=F32)
    two = lax.dot_general(a[1], e[base + depth + 1], nt, preferred_element_type=F32)
    if depth == 2:
        one = one * joined
    if depth == 0:
        two = two * joined
    g = one + two
    for k in range(9):
        tap = depth * 9 + k
        part[tap // SHARE, pl.ds((tap % SHARE) * N, N), :] = g[k * N : (k + 1) * N].astype(BF)


def filter_rows(rows, joined, depth, at, w):
    count = rows.shape[0]
    lanes = slice(depth * C, (depth + 1) * C)
    plain = rows.astype(BF)
    masked = (rows * joined).astype(BF)
    w[0, at : at + count, lanes] = masked if depth == 2 else plain
    w[1, at : at + count, lanes] = masked if depth == 0 else plain


def backward_filter(own, joined, w):
    for a in range(3):
        filter_rows(own[(2 - a) * 288 : (3 - a) * 288, :].astype(F32), joined, a, 0, w)


def whole(
    vol, cot, own1, own2,
    output, input_grad, g1, g2,
    e1, e2, e3, e4, w1, w2, t1, t2, wf1, wf2, wb1, wb2, s, pre, a1, a2, part1, part2,
    r1, p2, r2, q, rq, fin, send, recv,
):
    net = Net()
    barrier = pltpu.get_barrier_semaphore()
    greeted = [net.in_ring(t, core) for t in range(1, Y) for core in (0, 1)]
    greeted.append(net.in_ring(0, 1 - net.core))
    total = X * Z
    for t in range(1, Z):
        greeted.append(net.zdev(t))
        greeted.append(net.dev(((net.z + t) % Z) * X + net.x, net.y + 1 - 2 * net.yl, net.core))
    for t in range(1, X):
        greeted.append(net.xdev(t))
    for t in (1, -1):
        greeted.append(net.dev((net.q + t + total) % total, net.y, net.core))
    for device in greeted:
        pl.semaphore_signal(barrier, inc=1, device_id=device, device_id_type=MESH)

    base = 2 * net.yl
    joined = jnp.where(net.dp % 16 == 0, 0.0, 1.0).astype(F32)

    def own(e):
        return pl.ds(pl.multiple_of(net.c * N, N), N)

    gathers = []
    for i, e in enumerate((e1, e2, e3, e4)):
        cp = Copies(send, recv, (i % 2) * SEMS_GATHER)
        gathers.append(Gather(net, cp, e))
        assert cp.next == (i % 2 + 1) * SEMS_GATHER
    cp = Copies(send, recv, 2 * SEMS_GATHER)
    turn1 = Turn(net, cp, w1, t1, net.x, X, net.xdev)
    cp = Copies(send, recv, cp.next)
    turn2 = Turn(net, cp, w2, t2, net.z, Z, net.zdev)
    cp = Copies(send, recv, cp.next)
    red2 = Reduce(net, cp, part2, r1.at[1], p2.at[1], r2.at[1], q.at[1], rq.at[1], fin.at[1], g2)
    cp = Copies(send, recv, cp.next)
    red1 = Reduce(net, cp, part1, r1.at[0], p2.at[0], r2.at[0], q.at[0], rq.at[0], fin.at[0], g1)
    assert cp.next <= SEMS

    for j in (0, 1):
        e1[base + 1 + j, own(e1), :] = vol[j]
        p2[j, SHARE] = jnp.zeros((2, N, 128), BF)
    for part in (part1, part2):
        part[X - 1, pl.ds((SHARE - 1) * N, N), :] = jnp.zeros((N, C), BF)
    turn1.cut(own1)
    turn2.cut(own2)
    pl.semaphore_wait(barrier, len(greeted))
    inner, outer = 1 - net.yl, net.yl
    kinds = ((inner, "inner"), (outer, "outer"))
    turn1.start()
    gathers[0].start()
    turn2.start()
    gathers[0].step(1)
    backward_filter(own2, joined, wb2)
    gathers[0].step(2)
    turn1.spread()
    backward_filter(own1, joined, wb1)
    gathers[0].step(3)
    turn2.spread()
    gathers[0].step(4)
    turn1.finish()
    turn1.filters(joined, wf1)
    gathers[0].most()
    for j, kind in kinds:
        if kind == "outer":
            gathers[0].rest()
        v = conv(wf1, e1, base, s, 1, j)
        e2[base + 1 + j, own(e2), :] = jnp.where(v > 0, v, SLOPE * v).astype(BF)
        gathers[1].start((kind,))
        pre[j] = jnp.where(v > 0, jnp.float32(1.0), jnp.float32(SLOPE))
    gathers[0].cp.drain()

    gathers[1].step(1)
    gathers[1].step(2)
    turn2.finish()
    gathers[1].step(3)
    turn2.filters(joined, wf2)
    gathers[1].step(4)
    gathers[1].most()
    for j, kind in kinds:
        if kind == "outer":
            gathers[1].rest()
        v = conv(wf2, e2, base, s, 1, j)
        slope = jnp.where(v > 0, jnp.float32(1.0), jnp.float32(SLOPE))
        e3[base + 1 + j, own(e3), :] = (cot[j].astype(F32) * slope).astype(BF)
        gathers[2].start((kind,))
        output[j] = jnp.where(v > 0, v, SLOPE * v).astype(BF)
    gathers[1].cp.drain()

    grad_columns(e3, net.c, base, a2)
    gathers[2].step(1)
    grad_part(a2, e2, base, joined, 0, part2)
    gathers[2].step(2)
    grad_part(a2, e2, base, joined, 1, part2)
    gathers[2].step(3)
    grad_part(a2, e2, base, joined, 2, part2)
    red2.start()
    gathers[2].step(4)
    gathers[2].most()
    for j, kind in kinds:
        if kind == "outer":
            gathers[2].rest()
        v = conv(wb2, e3, base, s, -1, j)
        e4[base + 1 + j, own(e4), :] = (v * pre[j]).astype(BF)
        gathers[3].start((kind,))
    gathers[2].cp.drain()

    red2.sum_x()
    grad_columns(e4, net.c, base, a1)
    for depth in range(3):
        grad_part(a1, e1, base, joined, depth, part1)
    red1.start()
    gathers[3].step(1)
    gathers[3].step(2)
    red2.sum_z()
    red1.sum_x()
    gathers[3].step(3)
    gathers[3].step(4)
    red2.collect()
    red1.sum_z()
    gathers[3].most()
    input_grad[inner] = conv(wb1, e4, base, s, -1, inner).astype(BF)
    gathers[3].rest()
    red2.spread()
    red1.collect()
    input_grad[outer] = conv(wb1, e4, base, s, -1, outer).astype(BF)
    red1.spread()
    red2.finish()
    gathers[3].cp.drain()
    red1.finish()


SEMS_GATHER = 68
SEMS = 2 * SEMS_GATHER + 10 + 14 + 2 * 36


def local(volume, filter_one, filter_two, cotangent):
    def planes(v):
        return v.transpose(0, 3, 1, 2).reshape(2, N, HW)

    def back(v):
        return v.reshape(2, N, 32, 32).transpose(0, 2, 3, 1)

    vm = pl.BlockSpec(memory_space=pltpu.VMEM)
    shape = jax.ShapeDtypeStruct
    output, input_grad, g1, g2 = pl.pallas_call(
        whole,
        out_shape=(
            shape((2, N, HW), BF),
            shape((2, N, HW), BF),
            shape((TAPS * N, C), F32),
            shape((TAPS * N, C), F32),
        ),
        in_specs=[vm] * 4,
        out_specs=[vm] * 4,
        scratch_shapes=[
            pltpu.VMEM((6, C, HW), BF),
            pltpu.VMEM((6, C, HW), BF),
            pltpu.VMEM((6, C, HW), BF),
            pltpu.VMEM((6, C, HW), BF),
            pltpu.VMEM((8, N, C), BF),
            pltpu.VMEM((8, N, 128), BF),
            pltpu.VMEM((X, C, C), BF),
            pltpu.VMEM((Z, C, 128), BF),
            pltpu.VMEM((2, 288, 3 * C), BF),
            pltpu.VMEM((2, 288, 3 * C), BF),
            pltpu.VMEM((2, 288, 3 * C), BF),
            pltpu.VMEM((2, 288, 3 * C), BF),
            pltpu.VMEM((288, HW), F32),
            pltpu.VMEM((2, N, HW), F32),
            pltpu.VMEM((2, 288, HW), BF),
            pltpu.VMEM((2, 288, HW), BF),
            pltpu.VMEM((X, SHARE * N, C), BF),
            pltpu.VMEM((X, SHARE * N, C), BF),
            pltpu.VMEM((2, X - 1, SHARE * N, C), BF),
            pltpu.VMEM((2, Z, 2, N, 128), BF),
            pltpu.VMEM((2, 2 * Z - 1, N, 128), BF),
            pltpu.VMEM((2, 128, 128), BF),
            pltpu.VMEM((2, 8, N, 128), BF),
            pltpu.VMEM((2, X, Z, N, C), BF),
            pltpu.SemaphoreType.DMA((SEMS,)),
            pltpu.SemaphoreType.DMA((SEMS,)),
        ],
        compiler_params=pltpu.CompilerParams(
            collective_id=0, has_side_effects=True, vmem_limit_bytes=50 * 1024 * 1024
        ),
    )(
        planes(volume),
        planes(cotangent),
        filter_one.reshape(TAPS * N, C),
        filter_two.reshape(TAPS * N, C),
    )
    filters = (3, 3, 3, N, C)
    return back(output), back(input_grad), g1.reshape(filters), g2.reshape(filters)


def solution(mesh):
    rows = P("dp", None, None, "chan")
    filters = P(None, None, None, "chan", None)
    return jax.shard_map(
        local,
        mesh=mesh,
        in_specs=(rows, filters, filters, rows),
        out_specs=(rows, rows, filters, filters),
        check_vma=False,
    )
```
